32 devices in a mesh: node: 1, ep: 32 (over z, y, x, core).
Axes of the slice: x: 2, y: 2, z: 4, core: 2. Of those that a mesh axis runs over, the one named last changes fastest.
Arguments:
- images: bfloat16 [32, 257, 1280], P(('node', 'ep')), may hold values from -6 to 6
- w_query: bfloat16 [1280, 1280], P(None, 'node'), may hold values from -6 to 6
- w_key: bfloat16 [1280, 1280], P(None, 'node'), may hold values from -6 to 6
- w_value: bfloat16 [1280, 1280], P(None, 'node'), may hold values from -0.15625 to 0.15625
- w_output: bfloat16 [1280, 1280], replicated, may hold values from -0.15625 to 0.15625
- router: bfloat16 [1280, 32], replicated, may hold values from -0.15625 to 0.15625
- w_in: bfloat16 [32, 1280, 5120], P('ep', None, 'node'), may hold values from -0.15625 to 0.15625
- w_out: bfloat16 [32, 5120, 1280], P('ep', 'node'), may hold values from -0.078125 to 0.078125
- routes: int32 [32, 257, 2], P(('node', 'ep')), may hold values from 0 to 31, all different within a row; in each aligned block of 257 rows (0 to 256, 257 to 513, ..., all dimensions but the last counted through in order) at most 24 rows name the same one
Outputs:
- output: bfloat16 [32, 257, 1280], P(('node', 'ep'))
The draws below stay inside these ranges and needn't reach their ends.
Inputs may be any that keep to these rules, and one draw needn't show every extreme that they name: `routes`: the two experts of a token differ. At most 24 tokens of one image name the same expert, and in every draw some image has an expert named by exactly 24 of its tokens.
All inputs are finite; a program needn't handle non-finite values.
Results may differ from the reference program's by a relative error of at most 0.0085.
Values may be sent and summed in bfloat16 or wider, within the bound.
A program may use at most 128 MiB of HBM per device.

```python
import math
import jax
import jax.numpy as jnp
import numpy as np
from jax import lax

D = 1280
HEADS = 16
FF = 5120
TOK = 257
CAP = 24
EXPERTS = 32
IMAGES = 32
N_NODE = 1


def attention_pair(key):
    first_base = jnp.clip(jax.random.normal(jax.random.fold_in(key, 11), (D, D), jnp.float32), -4.0, 4.0)
    second_base = jnp.clip(jax.random.normal(jax.random.fold_in(key, 12), (D, D), jnp.float32), -4.0, 4.0)
    return (first_base, second_base)


def draw_w_query(key, part):
    first_base, second_base = attention_pair(key)
    values = first_base * D ** (-0.5)
    return values.astype(jnp.bfloat16)


def draw_w_key(key, part):
    first_base, second_base = attention_pair(key)
    values = second_base * D ** (-0.5)
    return values.astype(jnp.bfloat16)


def draw_images(key, part):
    shape = (IMAGES, TOK, D)
    values = jnp.clip(jax.random.normal(jax.random.fold_in(key, 23), shape, jnp.float32), -6.0, 6.0)
    return values.astype(jnp.bfloat16)


def levels(own_key, extent, shards, low, top_value):
    loudness, own = 1.0, jax.random.fold_in(own_key, 6)
    for axis_at, blocks in shards:
        heights = jnp.exp(jax.random.uniform(jax.random.fold_in(own, axis_at), (blocks,), jnp.float32, low / len(shards), top_value / len(shards)))
        loudness = loudness * jnp.repeat(heights, extent[axis_at] // blocks).reshape([-1 if axis == axis_at else 1 for axis in range(len(extent))])
    return loudness


def assign_block(key, own, number, rows, count, top, limit, lean):
    order = jax.random.permutation(key, count)
    heavy_load, common = portions_of(count, rows * top, limit, lean, True), portions_of(count, rows * top, limit, lean, False)
    places = jnp.arange(count)

    def named(tallies, turn):
        used = int((tallies > 0).sum())
        fixed = max(1, used // 4)
        passed = fixed + (places - fixed + turn * (used - fixed)) % max(1, count - fixed)
        return jnp.zeros((count,), jnp.int32).at[order[jnp.where(places < fixed, places, passed)]].set(jnp.asarray(tallies, jnp.int32))

    tallies = jnp.where(number % 4 == 0, named(heavy_load, number // 4), named(common, number - number // 4 - 1))
    mixed = jax.random.permutation(jax.random.fold_in(own, 3), count)
    donor, receiver = mixed[0:count // 2 * 2:2], mixed[1:count // 2 * 2:2]
    slack = jnp.minimum(tallies[donor] - 1, limit - tallies[receiver]) // 2
    slack = jnp.where((donor == order[0]) | (receiver == order[0]) | (tallies[receiver] == 0), 0, jnp.maximum(slack, 0))
    passed = jax.random.randint(jax.random.fold_in(own, 4), (count // 2,), 0, 1 << 20) % (slack + 1)
    tallies = tallies.at[donor].add(-passed).at[receiver].add(passed)
    labels = jnp.searchsorted(jnp.cumsum(tallies), jnp.arange(rows * top), side="right").astype(jnp.int32)
    grid = labels.reshape(top, rows).T
    grid = grid[jax.random.permutation(jax.random.fold_in(own, 1), rows)]
    turn = jax.random.randint(jax.random.fold_in(own, 2), (rows, 1), 0, top)
    return jnp.take_along_axis(grid, (jnp.arange(top)[None, :] + turn) % top, axis=1)


def portions_of(amount, total, most, lean, full):
    weights = [(1 << 20) // math.isqrt(grade ** lean) + 1 for grade in range(1, amount + 1)]
    largest = most if full else min(most, max(-(-total // amount), total * weights[0] // sum(weights)))
    least = 1 if total - largest >= amount - 1 else 0
    counts, surplus = [largest] + [least] * (amount - 1), total - largest - least * (amount - 1)
    while surplus > 0:
        candidates = [i for i in range(1, amount) if counts[i] < largest] or [i for i in range(1, amount) if counts[i] < most]
        pool, left = sum([weights[i] for i in candidates]), surplus
        for i in candidates:
            more = min(most - counts[i], max(1, left * weights[i] // pool), surplus)
            counts[i] = counts[i] + more
            surplus = surplus - more
    return np.array(counts)


def bell_draw(stream_key, shape, scale, limit, cuts=(), held_as=jnp.bfloat16):
    array = jax.random.normal(stream_key, shape, jnp.float32) * scale
    if len(cuts) > 0:
        array = levels(stream_key, shape, cuts, -0.22, 0.18) * array
    return jnp.clip(array, min=-limit, max=limit).astype(held_as)


def setup_inputs(seed: int = 0) -> dict:
    keys = jax.random.split(jax.random.key(seed), 10)
    images = draw_images(jax.random.fold_in(keys[9], 71), 0)
    w_query = draw_w_query(jax.random.fold_in(keys[9], 71), 0)
    w_key = draw_w_key(jax.random.fold_in(keys[9], 71), 0)
    w_value = bell_draw(keys[3], (D, D), D ** -0.5, 0.15625)
    w_output = bell_draw(keys[4], (D, D), D ** -0.5, 0.15625)
    router = bell_draw(keys[5], (D, EXPERTS), D ** -0.5, 0.15625)
    w_in = bell_draw(keys[6], (EXPERTS, D, FF), D ** -0.5, 0.15625, ((0, 32),))
    w_out = bell_draw(keys[7], (EXPERTS, FF, D), FF ** -0.5, 0.078125, ((0, 32),))
    routes_keys = jax.random.split(jax.random.fold_in(keys[8], 1), IMAGES * TOK // TOK)
    routes_turns = jax.random.permutation(jax.random.fold_in(keys[8], 3), IMAGES * TOK // TOK)
    routes = jax.vmap(lambda own, number: assign_block(jax.random.fold_in(keys[8], 2), own, number, TOK, EXPERTS, 2, CAP, 2))(routes_keys, routes_turns).reshape((IMAGES, TOK, 2))
    return dict(images=images, w_query=w_query, w_key=w_key, w_value=w_value, w_output=w_output, router=router, w_in=w_in, w_out=w_out, routes=routes)


def layer_norm(values):
    center = values - lax.optimization_barrier(jnp.mean(values, axis=-1, keepdims=True))
    spread = lax.optimization_barrier(jnp.mean(center * center, axis=-1, keepdims=True))
    return center * lax.rsqrt(spread + 1e-06)

def slot_table(chosen, num_experts):
    onehot = (chosen[..., None] == jnp.arange(num_experts, dtype=jnp.int32)).astype(jnp.int32)
    before = jnp.cumsum(onehot, axis=1) - onehot
    return lax.optimization_barrier(jnp.sum(before * onehot, axis=-1)).astype(jnp.int32)

def reference(images, w_query, w_key, w_value, w_output, router, w_in, w_out, routes):
    head_size = D // HEADS

    def attend_image(single):
        inputs = single.astype(jnp.float32)
        normed = layer_norm(inputs).astype(jnp.bfloat16)
        queries = jnp.dot(normed, w_query, preferred_element_type=jnp.float32).astype(jnp.bfloat16)
        projected_keys = jnp.dot(normed, w_key, preferred_element_type=jnp.float32).astype(jnp.bfloat16)
        projected_values = jnp.dot(normed, w_value, preferred_element_type=jnp.float32).astype(jnp.bfloat16)
        query_heads = queries.astype(jnp.float32).reshape(TOK, HEADS, head_size)
        key_heads = projected_keys.astype(jnp.float32).reshape(TOK, HEADS, head_size)
        value_heads = projected_values.astype(jnp.float32).reshape(TOK, HEADS, head_size)
        scores = jnp.einsum('qhd,khd->hqk', query_heads, key_heads) / math.sqrt(head_size)
        weights = jax.nn.softmax(scores, axis=-1).astype(jnp.bfloat16)
        mixture = jnp.einsum('hqk,khd->qhd', weights.astype(jnp.float32), value_heads)
        mixture = mixture.astype(jnp.bfloat16).reshape(TOK, D)
        return inputs + jnp.dot(mixture, w_output, preferred_element_type=jnp.float32)
    middle = lax.map(attend_image, images)
    normed = layer_norm(middle).astype(jnp.bfloat16)
    logits = jnp.einsum('itd,de->ite', normed.astype(jnp.float32), router.astype(jnp.float32))
    chosen_mask = routes[..., None] == jnp.arange(EXPERTS, dtype=jnp.int32)
    chosen_logit = lax.optimization_barrier(jnp.sum(jnp.where(chosen_mask, logits[:, :, None, :], jnp.float32(0.0)), axis=-1))
    gate_values = jax.nn.sigmoid(chosen_logit)
    flat_routes = routes.reshape(IMAGES, 2 * TOK)
    slot_index = slot_table(flat_routes, EXPERTS)
    per_expert = IMAGES * CAP
    image_base = jnp.arange(IMAGES, dtype=jnp.int32)[:, None] * CAP
    position = (flat_routes * per_expert + image_base + slot_index).reshape(-1).astype(jnp.int32)
    token_ids = jnp.arange(IMAGES * 2 * TOK, dtype=jnp.int32) // 2
    source = jnp.full((EXPERTS * per_expert,), -1, jnp.int32).at[position].set(token_ids)
    token_rows = normed.reshape(IMAGES * TOK, D)
    gathered = jnp.take(token_rows, jnp.maximum(source, 0), axis=0)
    gathered = jnp.where(source[:, None] >= 0, gathered, jnp.zeros_like(gathered))
    gathered = gathered.reshape(EXPERTS, per_expert, D)
    quarter = FF // N_NODE

    def run_expert(operands):
        buffer, first_weight, second_weight = operands
        summed = jnp.zeros((per_expert, D), jnp.float32)
        for section in range(N_NODE):
            pre_act = jnp.dot(buffer, first_weight[:, section * quarter:(section + 1) * quarter], preferred_element_type=jnp.float32)
            hidden = jax.nn.gelu(pre_act, approximate=True).astype(jnp.bfloat16)
            partial_sum = jnp.dot(hidden, second_weight[section * quarter:(section + 1) * quarter, :], preferred_element_type=jnp.float32).astype(jnp.bfloat16)
            summed = summed + lax.optimization_barrier(partial_sum).astype(jnp.float32)
        return summed.astype(jnp.bfloat16)
    results = lax.map(run_expert, (gathered, w_in, w_out))
    picked = jnp.take(results.reshape(EXPERTS * per_expert, D), position, axis=0).reshape(IMAGES, TOK, 2, D)
    expert_mix = lax.optimization_barrier(jnp.sum(gate_values[..., None] * picked.astype(jnp.float32), axis=2))
    return (middle + expert_mix).astype(jnp.bfloat16)
```

```python
import functools
import math

import jax
import jax.numpy as jnp
from jax import lax
from jax.experimental import pallas as pl
from jax.experimental.pallas import tpu as pltpu
from jax.sharding import PartitionSpec as P

HEAD = 80
CAP = 24
LANES = 128
TILE = 256
PLANES = 4
CHUNK = 8
VMEM_BYTES = 60 * 1024 * 1024
MESH = pl.DeviceIdType.MESH


def up_to(value, step):
    return (value + step - 1) // step * step


def layer_norm(values):
    center = values - jnp.mean(values, axis=-1, keepdims=True)
    spread = jnp.mean(center * center, axis=-1, keepdims=True)
    return center * lax.rsqrt(spread + 1e-06)


def choose(rows, experts, routes, table, which):
    columns = lax.broadcasted_iota(jnp.int32, (rows, experts), 1)
    return jnp.sum(jnp.where(routes[:, which : which + 1] == columns, table, 0.0), axis=1, keepdims=True)


def route(tokens, rows, wide, router_ref, routes_ref, middle, out_ref, gate_ref, place_ref, normed, wanted):
    width = middle.shape[1]
    experts = router_ref.shape[1]
    slots = experts * CAP
    normed[rows:, :] = jnp.zeros((wide - rows, width), jnp.bfloat16)
    normed[:rows, :] = layer_norm(middle[...]).astype(jnp.bfloat16)
    wanted[...] = jnp.full((wide, 2), -1, jnp.int32)
    wanted[:tokens, :] = routes_ref[0]
    routes_wide = wanted[...]
    routes = routes_wide[:rows, :]
    logits = jnp.dot(normed[:rows, :], router_ref[...], preferred_element_type=jnp.float32)
    columns = lax.broadcasted_iota(jnp.int32, (wide, experts), 1)
    named = jnp.where(routes_wide[:, 0:1] == columns, 1.0, 0.0) + jnp.where(
        routes_wide[:, 1:2] == columns, 1.0, 0.0
    )
    earlier = jnp.where(
        lax.broadcasted_iota(jnp.int32, (rows, wide), 1) < lax.broadcasted_iota(jnp.int32, (rows, wide), 0),
        1.0,
        0.0,
    ).astype(jnp.bfloat16)
    rank = jnp.dot(earlier, named.astype(jnp.bfloat16), preferred_element_type=jnp.float32)
    slot_of = lax.broadcasted_iota(jnp.int32, (rows, slots), 1)
    sends = jnp.zeros((rows, slots), jnp.float32)
    for which in range(2):
        chosen = choose(rows, experts, routes, logits, which)
        gate_ref[:, which : which + 1] = jax.nn.sigmoid(chosen)
        turn = choose(rows, experts, routes, rank, which).astype(jnp.int32)
        place = routes[:, which : which + 1] * CAP + turn
        place_ref[:, which : which + 1] = place
        sends = sends + jnp.where(place == slot_of, 1.0, 0.0)
    sends = jnp.concatenate([sends, jnp.zeros((wide - rows, slots), jnp.float32)], axis=0)
    picks = jnp.transpose(sends).astype(jnp.bfloat16)

    @pl.loop(0, width // TILE)
    def _(tile):
        part = pl.ds(pl.multiple_of(tile * TILE, TILE), TILE)
        block = jnp.dot(picks, normed[:, part], preferred_element_type=jnp.float32)
        out_ref[:, :, part] = block.reshape(experts, CAP, TILE).astype(jnp.bfloat16)


def attend_kernel(
    tokens, images_ref, q_hbm, k_hbm, v_hbm, o_hbm, router_ref, routes_ref,
    out_ref, middle_ref, gate_ref, place_ref,
    weights, sems, inputs, normed, queries, keys, values, mixed, second, wanted,
):
    rows, width = inputs.shape
    wide = keys.shape[0]
    loads = [
        pltpu.make_async_copy(source, weights.at[at], sems.at[at])
        for at, source in enumerate((q_hbm, k_hbm, v_hbm, o_hbm))
    ]
    for load in loads:
        load.start()
    inputs[...] = jnp.zeros((rows, width), jnp.float32)
    inputs[:tokens, :] = images_ref[0].astype(jnp.float32)
    normed[...] = layer_norm(inputs[...]).astype(jnp.bfloat16)
    mixed[...] = jnp.zeros((rows, width), jnp.float32)
    keys[rows:, :] = jnp.zeros((wide - rows, width), jnp.bfloat16)
    values[rows:, :] = jnp.zeros((wide - rows, width), jnp.bfloat16)
    for at, target in enumerate((queries, keys, values)):
        loads[at].wait()

        @pl.loop(0, width // TILE)
        def _(tile):
            part = pl.ds(pl.multiple_of(tile * TILE, TILE), TILE)
            target[:rows, part] = jnp.dot(
                normed[...], weights[at, :, part], preferred_element_type=jnp.float32
            ).astype(jnp.bfloat16)

    period = math.lcm(HEAD, LANES)
    valid = lax.broadcasted_iota(jnp.int32, (rows, wide), 1) < tokens

    @pl.loop(0, width // period)
    def _(turn):
        for head in range(period // HEAD):
            low = head * HEAD // LANES * LANES
            span = up_to(head * HEAD + HEAD, LANES) - low
            part = pl.ds(pl.multiple_of(turn * period + low, LANES), span)
            lane = lax.broadcasted_iota(jnp.int32, (rows, span), 1) + low
            inside = (lane >= head * HEAD) & (lane < head * HEAD + HEAD)
            query = jnp.where(inside, queries[:, part].astype(jnp.float32), 0.0).astype(jnp.bfloat16)
            scores = lax.dot_general(
                query, keys[:, part], (((1,), (1,)), ((), ())), preferred_element_type=jnp.float32
            ) * (1.0 / math.sqrt(HEAD))
            scores = jnp.where(valid, scores, -1e30)
            raised = jnp.exp(scores - jnp.max(scores, axis=1, keepdims=True))
            raised = jnp.where(valid, raised, 0.0)
            probs = (raised * (1.0 / jnp.sum(raised, axis=1, keepdims=True))).astype(jnp.bfloat16)
            result = jnp.dot(probs, values[:, part], preferred_element_type=jnp.float32)
            mixed[:, part] += jnp.where(inside, result, 0.0)

    normed[...] = mixed[...].astype(jnp.bfloat16)
    loads[3].wait()

    @pl.loop(0, width // TILE)
    def _(tile):
        part = pl.ds(pl.multiple_of(tile * TILE, TILE), TILE)
        middle_ref[:, part] = inputs[:, part] + jnp.dot(
            normed[...], weights[3, :, part], preferred_element_type=jnp.float32
        )

    route(tokens, rows, wide, router_ref, routes_ref, middle_ref, out_ref, gate_ref, place_ref, second, wanted)


def route_kernel(tokens, middle_ref, router_ref, routes_ref, out_ref, gate_ref, place_ref, second, wanted):
    rows, wide = middle_ref.shape[0], second.shape[0]
    route(tokens, rows, wide, router_ref, routes_ref, middle_ref, out_ref, gate_ref, place_ref, second, wanted)


def expert_kernel(
    node_count, columns, out_ref, in_hbm, down_hbm, back_ref,
    first, second, arrived, results, total, weight_sems, go_send, go_recv, back_send, back_recv,
):
    number = node_count * columns
    plane = number // PLANES
    chunks = number // CHUNK
    own_slot = 4
    me = lax.axis_index("node") * columns + lax.axis_index("ep")
    loads = [
        pltpu.make_async_copy(in_hbm.at[0], first, weight_sems.at[0]),
        pltpu.make_async_copy(down_hbm.at[0], second, weight_sems.at[1]),
    ]
    for load in loads:
        load.start()

    def offset(slot):
        within = slot % CHUNK
        return (within // 2 + 2) % PLANES * plane + slot // CHUNK * 2 + within % 2

    def name(device):
        return (device // columns, device % columns)

    def go(slot):
        target = (me + offset(slot)) % number
        return pltpu.make_async_remote_copy(
            src_ref=out_ref.at[target % columns],
            dst_ref=arrived.at[slot],
            send_sem=go_send.at[slot],
            recv_sem=go_recv.at[slot],
            device_id=name(target),
            device_id_type=MESH,
        )

    def back(slot):
        source = (me - offset(slot) + number) % number
        return pltpu.make_async_remote_copy(
            src_ref=results.at[slot],
            dst_ref=back_ref.at[me],
            send_sem=back_send.at[slot],
            recv_sem=back_recv.at[slot],
            device_id=name(source),
            device_id_type=MESH,
        )

    def landed(slot):
        source = (me + offset(slot)) % number
        return pltpu.make_async_remote_copy(
            src_ref=results.at[slot],
            dst_ref=back_ref.at[source],
            send_sem=back_send.at[slot],
            recv_sem=back_recv.at[slot],
            device_id=name(source),
            device_id_type=MESH,
        )

    barrier = pltpu.get_barrier_semaphore()

    @pl.loop(1, number)
    def _(step):
        pl.semaphore_signal(barrier, inc=1, device_id=name((me + step) % number), device_id_type=MESH)

    pl.semaphore_wait(barrier, number - 1)

    @pl.loop(0, number)
    def _(slot):
        @pl.when(slot != own_slot)
        def _():
            go(slot).start()

    arrived[own_slot] = out_ref[me % columns]
    for load in loads:
        load.wait()
    width, hidden_units = first.shape
    section = width if hidden_units % width == 0 else hidden_units

    @pl.loop(0, chunks)
    def _(chunk):
        for within in range(CHUNK):
            slot = chunk * CHUNK + within

            @pl.when(slot != own_slot)
            def _():
                go(slot).wait_recv()

        held = pl.ds(chunk * CHUNK, CHUNK)
        buffer = arrived[held].astype(jnp.float32).reshape(CHUNK * CAP, width).astype(jnp.bfloat16)
        total[...] = jnp.zeros_like(total)

        @pl.loop(0, hidden_units // section)
        def _(at):
            part = pl.ds(pl.multiple_of(at * section, section), section)
            before = jnp.dot(buffer, first[:, part], preferred_element_type=jnp.float32)
            hidden = jax.nn.gelu(before, approximate=True).astype(jnp.bfloat16)
            total[...] += jnp.dot(hidden, second[part, :], preferred_element_type=jnp.float32)

        results[held] = total[...].reshape(CHUNK, CAP, width).astype(jnp.bfloat16)
        for within in range(CHUNK):
            slot = chunk * CHUNK + within

            @pl.when(slot != own_slot)
            def _():
                back(slot).start()

    back_ref[me] = results[own_slot]

    @pl.loop(0, number)
    def _(slot):
        @pl.when(slot != own_slot)
        def _():
            go(slot).wait_send()
            back(slot).wait_send()
            landed(slot).wait_recv()


def combine_kernel(tokens, middle_ref, gate_ref, place_ref, back_ref, out_ref):
    rows, width = middle_ref.shape
    experts = back_ref.shape[0]
    slots = experts * CAP
    slot_of = lax.broadcasted_iota(jnp.int32, (rows, slots), 1)
    picks = [
        jnp.where(place_ref[:, which : which + 1] == slot_of, 1.0, 0.0).astype(jnp.bfloat16)
        for which in range(2)
    ]

    @pl.loop(0, width // TILE)
    def _(tile):
        part = pl.ds(pl.multiple_of(tile * TILE, TILE), TILE)
        block = back_ref[:, :, part].astype(jnp.float32).reshape(slots, TILE).astype(jnp.bfloat16)
        value = middle_ref[:, part]
        mix = jnp.zeros_like(value)
        for which in range(2):
            mix = mix + gate_ref[:, which : which + 1] * jnp.dot(
                picks[which], block, preferred_element_type=jnp.float32
            )
        out_ref[0, :, part] = (value + mix)[:tokens, :].astype(jnp.bfloat16)


def attention_over_nodes(images, w_query, w_key, w_value, w_output):
    local_heads = w_query.shape[1] // HEAD
    inputs = images.astype(jnp.float32)
    normed = layer_norm(inputs).astype(jnp.bfloat16)
    gathered = lax.all_gather(normed, "node", axis=0, tiled=True)
    number, tokens, _ = gathered.shape

    def project(weight):
        result = jnp.einsum("ctd,de->cte", gathered, weight, preferred_element_type=jnp.float32)
        return result.astype(jnp.bfloat16).reshape(number, tokens, local_heads, HEAD)

    scores = jnp.einsum(
        "cqhd,ckhd->chqk", project(w_query), project(w_key), preferred_element_type=jnp.float32
    ) / math.sqrt(HEAD)
    probs = jax.nn.softmax(scores, axis=-1).astype(jnp.bfloat16)
    mixture = jnp.einsum(
        "chqk,ckhd->cqhd", probs, project(w_value), preferred_element_type=jnp.float32
    ).astype(jnp.bfloat16)
    mixture = mixture.reshape(number, tokens, local_heads * HEAD)
    mixture = lax.all_to_all(mixture, "node", split_axis=0, concat_axis=2, tiled=True)
    return inputs + jnp.einsum("itd,de->ite", mixture, w_output, preferred_element_type=jnp.float32)


def shards(images, w_query, w_key, w_value, w_output, router, w_in, w_out, routes):
    _, tokens, width = images.shape
    node_count = lax.axis_size("node")
    columns = lax.axis_size("ep")
    number = node_count * columns
    experts = router.shape[1]
    hidden_units = w_in.shape[2]
    rows, wide = up_to(tokens, 16), up_to(tokens, LANES)
    here = pl.BlockSpec(memory_space=pltpu.VMEM)
    anywhere = pl.BlockSpec(memory_space=pl.ANY)
    params = pltpu.CompilerParams(vmem_limit_bytes=VMEM_BYTES)
    blocks = jax.ShapeDtypeStruct((experts, CAP, width), jnp.bfloat16)
    middle_shape = jax.ShapeDtypeStruct((rows, width), jnp.float32)
    small = [jax.ShapeDtypeStruct((rows, 2), jnp.float32), jax.ShapeDtypeStruct((rows, 2), jnp.int32)]
    route_scratch = [pltpu.VMEM((wide, width), jnp.bfloat16), pltpu.VMEM((wide, 2), jnp.int32)]
    if node_count == 1:
        outgoing, middle, gates, places = pl.pallas_call(
            functools.partial(attend_kernel, tokens),
            out_shape=[blocks, middle_shape] + small,
            in_specs=[here] + [anywhere] * 4 + [here] * 2,
            out_specs=[here] * 4,
            scratch_shapes=[
                pltpu.VMEM((4, width, width), jnp.bfloat16),
                pltpu.SemaphoreType.DMA((4,)),
                pltpu.VMEM((rows, width), jnp.float32),
                pltpu.VMEM((rows, width), jnp.bfloat16),
                pltpu.VMEM((rows, width), jnp.bfloat16),
                pltpu.VMEM((wide, width), jnp.bfloat16),
                pltpu.VMEM((wide, width), jnp.bfloat16),
                pltpu.VMEM((rows, width), jnp.float32),
            ] + route_scratch,
            compiler_params=params,
            name="attend",
        )(images, w_query, w_key, w_value, w_output, router, routes)
    else:
        middle = attention_over_nodes(images, w_query, w_key, w_value, w_output)[0]
        middle = jnp.pad(middle, ((0, rows - tokens), (0, 0)))
        outgoing, gates, places = pl.pallas_call(
            functools.partial(route_kernel, tokens),
            out_shape=[blocks] + small,
            in_specs=[here] * 3,
            out_specs=[here] * 3,
            scratch_shapes=route_scratch,
            compiler_params=params,
            name="route",
        )(middle, router, routes)
    returned = pl.pallas_call(
        functools.partial(expert_kernel, node_count, columns),
        out_shape=jax.ShapeDtypeStruct((number, CAP, width), jnp.bfloat16),
        in_specs=[here, anywhere, anywhere],
        out_specs=here,
        scratch_shapes=[
            pltpu.VMEM((width, hidden_units), jnp.bfloat16),
            pltpu.VMEM((hidden_units, width), jnp.bfloat16),
            pltpu.VMEM((number, CAP, width), jnp.bfloat16),
            pltpu.VMEM((number, CAP, width), jnp.bfloat16),
            pltpu.VMEM((CHUNK * CAP, width), jnp.float32),
            pltpu.SemaphoreType.DMA((2,)),
            pltpu.SemaphoreType.DMA((number,)),
            pltpu.SemaphoreType.DMA((number,)),
            pltpu.SemaphoreType.DMA((number,)),
            pltpu.SemaphoreType.DMA((number,)),
        ],
        compiler_params=pltpu.CompilerParams(
            collective_id=0, has_side_effects=True, vmem_limit_bytes=VMEM_BYTES
        ),
        name="experts",
    )(outgoing, w_in, w_out)
    if node_count > 1:
        summed = jnp.sum(returned.astype(jnp.float32).reshape(node_count, experts, CAP, width), axis=0)
        returned = summed.astype(jnp.bfloat16)
    return pl.pallas_call(
        functools.partial(combine_kernel, tokens),
        out_shape=jax.ShapeDtypeStruct(images.shape, jnp.bfloat16),
        in_specs=[here] * 4,
        out_specs=here,
        compiler_params=params,
        name="combine",
    )(middle, gates, places, returned)


def solution(mesh):
    placed = (
        P(("node", "ep"), None, None),
        P(None, "node"),
        P(None, "node"),
        P(None, "node"),
        P(),
        P(),
        P("ep", None, "node"),
        P("ep", "node", None),
        P(("node", "ep"), None, None),
    )
    return jax.shard_map(
        shards, mesh=mesh, in_specs=placed, out_specs=P(("node", "ep"), None, None), check_vma=False
    )
```

```python
import functools
import math

import jax
import jax.numpy as jnp
from jax import lax
from jax.experimental import pallas as pl
from jax.experimental.pallas import tpu as pltpu
from jax.sharding import PartitionSpec as P

HEAD = 80
CAP = 24
LANES = 128
TILE = 256
PLANES = 4
CHUNK = 8
VMEM_BYTES = 60 * 1024 * 1024
MESH = pl.DeviceIdType.MESH


def up_to(value, step):
    return (value + step - 1) // step * step


def layer_norm(values):
    center = values - jnp.mean(values, axis=-1, keepdims=True)
    spread = jnp.mean(center * center, axis=-1, keepdims=True)
    return center * lax.rsqrt(spread + 1e-06)


def choose(rows, experts, routes, table, which):
    columns = lax.broadcasted_iota(jnp.int32, (rows, experts), 1)
    return jnp.sum(jnp.where(routes[:, which : which + 1] == columns, table, 0.0), axis=1, keepdims=True)


def route(tokens, rows, wide, router_ref, routes_ref, middle, out_ref, gate_ref, place_ref, normed, wanted, turned=None):
    width = middle.shape[1]
    experts = router_ref.shape[0]
    slots = experts * CAP
    normed[rows:, :] = jnp.zeros((wide - rows, width), jnp.bfloat16)
    normed[:rows, :] = layer_norm(middle[...]).astype(jnp.bfloat16)
    wanted[...] = jnp.full(wanted.shape, -1.0, jnp.float32)
    wanted[0:2, :tokens] = routes_ref[...].astype(jnp.float32)
    routes_wide = jnp.transpose(wanted[...]).astype(jnp.int32)
    routes = routes_wide[:rows, :]
    logits = lax.dot_general(
        normed[:rows, :], router_ref[...], (((1,), (1,)), ((), ())), preferred_element_type=jnp.float32
    )
    columns = lax.broadcasted_iota(jnp.int32, (wide, experts), 1)
    named = jnp.where(routes_wide[:, 0:1] == columns, 1.0, 0.0) + jnp.where(
        routes_wide[:, 1:2] == columns, 1.0, 0.0
    )
    earlier = jnp.where(
        lax.broadcasted_iota(jnp.int32, (rows, wide), 1) < lax.broadcasted_iota(jnp.int32, (rows, wide), 0),
        1.0,
        0.0,
    ).astype(jnp.bfloat16)
    rank = jnp.dot(earlier, named.astype(jnp.bfloat16), preferred_element_type=jnp.float32)
    slot_of = lax.broadcasted_iota(jnp.int32, (rows, slots), 1)
    sends = jnp.zeros((rows, slots), jnp.float32)
    for which in range(2):
        chosen = choose(rows, experts, routes, logits, which)
        gate_ref[:, which : which + 1] = jax.nn.sigmoid(chosen)
        turn = choose(rows, experts, routes, rank, which).astype(jnp.int32)
        place = routes[:, which : which + 1] * CAP + turn
        kept = place
        if turned is not None:
            kept = turned(routes[:, which : which + 1]) * CAP + turn
        place_ref[:, which : which + 1] = kept
        sends = sends + jnp.where(place == slot_of, 1.0, 0.0)
    sends = jnp.concatenate([sends, jnp.zeros((wide - rows, slots), jnp.float32)], axis=0)
    picks = jnp.transpose(sends).astype(jnp.bfloat16)

    @pl.loop(0, width // TILE)
    def _(tile):
        part = pl.ds(pl.multiple_of(tile * TILE, TILE), TILE)
        block = jnp.dot(picks, normed[:, part], preferred_element_type=jnp.float32)
        out_ref[:, :, part] = block.reshape(experts, CAP, TILE).astype(jnp.bfloat16)


def attend(tokens, images_ref, loads, weights, middle_ref, inputs, normed, queries, keys, values, mixed):
    rows, width = inputs.shape
    wide = keys.shape[0]
    inputs[...] = jnp.zeros((rows, width), jnp.float32)
    inputs[:tokens, :] = images_ref[0].astype(jnp.float32)
    normed[...] = layer_norm(inputs[...]).astype(jnp.bfloat16)
    mixed[...] = jnp.zeros((rows, width), jnp.float32)
    keys[rows:, :] = jnp.zeros((wide - rows, width), jnp.bfloat16)
    values[rows:, :] = jnp.zeros((wide - rows, width), jnp.bfloat16)
    for at, target in enumerate((queries, keys, values)):
        loads[at].wait()

        @pl.loop(0, width // TILE)
        def _(tile):
            part = pl.ds(pl.multiple_of(tile * TILE, TILE), TILE)
            taken = pl.ds(pl.multiple_of(at * width + tile * TILE, TILE), TILE)
            target[:rows, part] = jnp.dot(
                normed[...], weights[:, taken], preferred_element_type=jnp.float32
            ).astype(jnp.bfloat16)

    period = math.lcm(HEAD, LANES)
    valid = lax.broadcasted_iota(jnp.int32, (rows, wide), 1) < tokens

    @pl.loop(0, width // period)
    def _(turn):
        for head in range(period // HEAD):
            low = head * HEAD // LANES * LANES
            span = up_to(head * HEAD + HEAD, LANES) - low
            part = pl.ds(pl.multiple_of(turn * period + low, LANES), span)
            lane = lax.broadcasted_iota(jnp.int32, (rows, span), 1) + low
            inside = (lane >= head * HEAD) & (lane < head * HEAD + HEAD)
            query = jnp.where(inside, queries[:, part].astype(jnp.float32), 0.0).astype(jnp.bfloat16)
            scores = lax.dot_general(
                query, keys[:, part], (((1,), (1,)), ((), ())), preferred_element_type=jnp.float32
            ) * (1.0 / math.sqrt(HEAD))
            scores = jnp.where(valid, scores, -1e30)
            raised = jnp.exp(scores - jnp.max(scores, axis=1, keepdims=True))
            raised = jnp.where(valid, raised, 0.0)
            probs = (raised * (1.0 / jnp.sum(raised, axis=1, keepdims=True))).astype(jnp.bfloat16)
            result = jnp.dot(probs, values[:, part], preferred_element_type=jnp.float32)
            mixed[:, part] += jnp.where(inside, result, 0.0)

    normed[...] = mixed[...].astype(jnp.bfloat16)
    loads[3].wait()

    @pl.loop(0, width // TILE)
    def _(tile):
        part = pl.ds(pl.multiple_of(tile * TILE, TILE), TILE)
        taken = pl.ds(pl.multiple_of(3 * width + tile * TILE, TILE), TILE)
        middle_ref[:, part] = inputs[:, part] + jnp.dot(
            normed[...], weights[:, taken], preferred_element_type=jnp.float32
        )


def route_kernel(tokens, middle_ref, router_ref, routes_ref, out_ref, gate_ref, place_ref, second, wanted):
    rows, wide = middle_ref.shape[0], second.shape[0]
    route(tokens, rows, wide, router_ref, routes_ref, middle_ref, out_ref, gate_ref, place_ref, second, wanted)


def place_of(node_count, columns):
    return lax.axis_index("node") * columns + lax.axis_index("ep")


def greet(node_count, columns):
    number = node_count * columns
    me = place_of(node_count, columns)
    barrier = pltpu.get_barrier_semaphore()

    @pl.loop(1, number)
    def _(step):
        peer = (me + step) % number
        pl.semaphore_signal(
            barrier, inc=1, device_id=(peer // columns, peer % columns), device_id_type=MESH
        )

    return lambda: pl.semaphore_wait(barrier, number - 1)


def exchange(
    node_count, columns, out_ref, loads, back_ref,
    first, second, arrived, results, total, go_send, go_recv, back_send, back_recv, taken=None,
):
    number = node_count * columns
    plane = number // PLANES
    chunks = number // CHUNK
    own_slot = 4
    me = place_of(node_count, columns)

    def offset(slot):
        within = slot % CHUNK
        return (within // 2 + 2) % PLANES * plane + slot // CHUNK * 2 + within % 2

    def name(device):
        return (device // columns, device % columns)

    def go(slot):
        target = (me + offset(slot)) % number
        return pltpu.make_async_remote_copy(
            src_ref=out_ref.at[target % columns],
            dst_ref=arrived.at[slot],
            send_sem=go_send.at[slot],
            recv_sem=go_recv.at[slot],
            device_id=name(target),
            device_id_type=MESH,
        )

    def back(slot):
        source = (me - offset(slot) + number) % number
        return pltpu.make_async_remote_copy(
            src_ref=results.at[slot],
            dst_ref=back_ref.at[slot],
            send_sem=back_send.at[slot],
            recv_sem=back_recv.at[slot],
            device_id=name(source),
            device_id_type=MESH,
        )

    def landed(slot):
        source = (me + offset(slot)) % number
        return pltpu.make_async_remote_copy(
            src_ref=results.at[slot],
            dst_ref=back_ref.at[slot],
            send_sem=back_send.at[slot],
            recv_sem=back_recv.at[slot],
            device_id=name(source),
            device_id_type=MESH,
        )

    @pl.loop(0, number)
    def _(slot):
        @pl.when(slot != own_slot)
        def _():
            go(slot).start()

    arrived[own_slot] = out_ref[me % columns]
    for load in loads:
        load.wait()
    width, hidden_units = first.shape
    section = width if hidden_units % width == 0 else hidden_units

    @pl.loop(0, chunks)
    def _(chunk):
        for within in range(CHUNK):
            slot = chunk * CHUNK + within

            @pl.when(slot != own_slot)
            def _():
                go(slot).wait_recv()

        held = pl.ds(chunk * CHUNK, CHUNK)
        buffer = arrived[held].astype(jnp.float32).reshape(CHUNK * CAP, width).astype(jnp.bfloat16)
        total[...] = jnp.zeros_like(total)

        @pl.loop(0, hidden_units // section)
        def _(at):
            part = pl.ds(pl.multiple_of(at * section, section), section)
            before = jnp.dot(buffer, first[:, part], preferred_element_type=jnp.float32)
            hidden = jax.nn.gelu(before, approximate=True).astype(jnp.bfloat16)
            total[...] += jnp.dot(hidden, second[part, :], preferred_element_type=jnp.float32)

        results[held] = total[...].reshape(CHUNK, CAP, width).astype(jnp.bfloat16)
        for within in range(CHUNK):
            slot = chunk * CHUNK + within

            @pl.when(slot != own_slot)
            def _():
                back(slot).start()

    back_ref[own_slot] = results[own_slot]

    @pl.loop(0, chunks)
    def _(chunk):
        for within in range(CHUNK):
            slot = chunk * CHUNK + within

            @pl.when(slot != own_slot)
            def _():
                landed(slot).wait_recv()

        if taken is not None:
            taken(chunk)

    @pl.loop(0, number)
    def _(slot):
        @pl.when(slot != own_slot)
        def _():
            go(slot).wait_send()
            back(slot).wait_send()


def slot_for(expert, me, columns):
    plane = columns // PLANES
    away = (expert - me + columns) & (columns - 1)
    ahead, step = away // plane, away & (plane - 1)
    return step // 2 * CHUNK + ((ahead + PLANES - 2) & (PLANES - 1)) * 2 + (step & 1)


def layer_kernel(
    tokens, columns, images_ref, q_hbm, k_hbm, v_hbm, o_hbm, router_ref, routes_ref, in_hbm, down_hbm, result_ref,
    first, second, outgoing, arrived, results, returned, total, middle, gates, places,
    inputs, normed, queries, keys, values, mixed, normed_second, wanted,
    load_sems, go_send, go_recv, back_send, back_recv,
):
    rows, width = inputs.shape
    wide = keys.shape[0]
    loads = [
        pltpu.make_async_copy(source, first.at[:, pl.ds(at * width, width)], load_sems.at[at])
        for at, source in enumerate((q_hbm, k_hbm, v_hbm, o_hbm))
    ]
    for load in loads:
        load.start()
    down = pltpu.make_async_copy(down_hbm.at[0], second, load_sems.at[4])
    up = pltpu.make_async_copy(in_hbm.at[0], first, load_sems.at[5])
    down.start()
    met = greet(1, columns)
    attend(tokens, images_ref, loads, first, middle, inputs, normed, queries, keys, values, mixed)
    up.start()
    me = place_of(1, columns)
    route(
        tokens, rows, wide, router_ref, routes_ref, middle, outgoing, gates, places, normed_second, wanted,
        lambda expert: slot_for(expert, me, columns),
    )
    met()
    span = CHUNK * CAP

    def taken(chunk):
        column = lax.broadcasted_iota(jnp.int32, (rows, span), 1) + chunk * span
        picks = [
            jnp.where(places[:, which : which + 1] == column, 1.0, 0.0).astype(jnp.bfloat16)
            for which in range(2)
        ]
        blocks = returned[pl.ds(chunk * CHUNK, CHUNK)].astype(jnp.float32)
        blocks = blocks.reshape(span, width).astype(jnp.bfloat16)
        for tile in range(width // TILE):
            part = pl.ds(tile * TILE, TILE)
            mix = middle[:, part]
            for which in range(2):
                mix = mix + gates[:, which : which + 1] * jnp.dot(
                    picks[which], blocks[:, tile * TILE : (tile + 1) * TILE], preferred_element_type=jnp.float32
                )
            middle[:, part] = mix

    exchange(
        1, columns, outgoing, [down, up], returned,
        first, second, arrived, results, total, go_send, go_recv, back_send, back_recv, taken,
    )
    result_ref[0] = middle[:tokens, :].astype(jnp.bfloat16)


def expert_kernel(
    node_count, columns, out_ref, in_hbm, down_hbm, back_ref,
    first, second, arrived, results, total, load_sems, go_send, go_recv, back_send, back_recv,
):
    loads = [
        pltpu.make_async_copy(in_hbm.at[0], first, load_sems.at[0]),
        pltpu.make_async_copy(down_hbm.at[0], second, load_sems.at[1]),
    ]
    for load in loads:
        load.start()
    greet(node_count, columns)()
    exchange(
        node_count, columns, out_ref, loads, back_ref,
        first, second, arrived, results, total, go_send, go_recv, back_send, back_recv,
    )


def combine_kernel(tokens, middle_ref, gate_ref, place_ref, back_ref, out_ref):
    rows, width = middle_ref.shape
    experts = back_ref.shape[0]
    slots = experts * CAP
    slot_of = lax.broadcasted_iota(jnp.int32, (rows, slots), 1)
    picks = [
        jnp.where(place_ref[:, which : which + 1] == slot_of, 1.0, 0.0).astype(jnp.bfloat16)
        for which in range(2)
    ]

    @pl.loop(0, width // TILE)
    def _(tile):
        part = pl.ds(pl.multiple_of(tile * TILE, TILE), TILE)
        block = back_ref[:, :, part].astype(jnp.float32).reshape(slots, TILE).astype(jnp.bfloat16)
        value = middle_ref[:, part]
        mix = jnp.zeros_like(value)
        for which in range(2):
            mix = mix + gate_ref[:, which : which + 1] * jnp.dot(
                picks[which], block, preferred_element_type=jnp.float32
            )
        out_ref[0, :, part] = (value + mix)[:tokens, :].astype(jnp.bfloat16)


def attention_over_nodes(images, w_query, w_key, w_value, w_output):
    local_heads = w_query.shape[1] // HEAD
    inputs = images.astype(jnp.float32)
    normed = layer_norm(inputs).astype(jnp.bfloat16)
    gathered = lax.all_gather(normed, "node", axis=0, tiled=True)
    number, tokens, _ = gathered.shape

    def project(weight):
        result = jnp.einsum("ctd,de->cte", gathered, weight, preferred_element_type=jnp.float32)
        return result.astype(jnp.bfloat16).reshape(number, tokens, local_heads, HEAD)

    scores = jnp.einsum(
        "cqhd,ckhd->chqk", project(w_query), project(w_key), preferred_element_type=jnp.float32
    ) / math.sqrt(HEAD)
    probs = jax.nn.softmax(scores, axis=-1).astype(jnp.bfloat16)
    mixture = jnp.einsum(
        "chqk,ckhd->cqhd", probs, project(w_value), preferred_element_type=jnp.float32
    ).astype(jnp.bfloat16)
    mixture = mixture.reshape(number, tokens, local_heads * HEAD)
    mixture = lax.all_to_all(mixture, "node", split_axis=0, concat_axis=2, tiled=True)
    return inputs + jnp.einsum("itd,de->ite", mixture, w_output, preferred_element_type=jnp.float32)


def shards(images, w_query, w_key, w_value, w_output, router, w_in, w_out, routes):
    _, tokens, width = images.shape
    node_count = lax.axis_size("node")
    columns = lax.axis_size("ep")
    number = node_count * columns
    experts = router.shape[1]
    hidden_units = w_in.shape[2]
    rows, wide = up_to(tokens, 16), up_to(tokens, LANES)
    here = pl.BlockSpec(memory_space=pltpu.VMEM)
    anywhere = pl.BlockSpec(memory_space=pl.ANY)
    params = pltpu.CompilerParams(vmem_limit_bytes=VMEM_BYTES)
    blocks = jax.ShapeDtypeStruct((experts, CAP, width), jnp.bfloat16)
    middle_shape = jax.ShapeDtypeStruct((rows, width), jnp.float32)
    small = [jax.ShapeDtypeStruct((rows, 2), jnp.float32), jax.ShapeDtypeStruct((rows, 2), jnp.int32)]
    route_scratch = [pltpu.VMEM((wide, width), jnp.bfloat16), pltpu.VMEM((8, wide), jnp.float32)]
    exchange_blocks = pltpu.VMEM((number, CAP, width), jnp.bfloat16)
    weight_scratch = [
        pltpu.VMEM((width, hidden_units), jnp.bfloat16),
        pltpu.VMEM((hidden_units, width), jnp.bfloat16),
    ]
    total_scratch = pltpu.VMEM((CHUNK * CAP, width), jnp.float32)
    remote_sems = [pltpu.SemaphoreType.DMA((number,))] * 4
    remote_params = pltpu.CompilerParams(
        collective_id=0, has_side_effects=True, vmem_limit_bytes=VMEM_BYTES
    )
    router_rows, route_rows = router.T, routes[0].T
    if node_count == 1 and hidden_units >= 4 * width:
        return pl.pallas_call(
            functools.partial(layer_kernel, tokens, columns),
            out_shape=jax.ShapeDtypeStruct(images.shape, jnp.bfloat16),
            in_specs=[here] + [anywhere] * 4 + [here] * 2 + [anywhere] * 2,
            out_specs=here,
            scratch_shapes=weight_scratch + [exchange_blocks] * 4 + [
                total_scratch,
                pltpu.VMEM((rows, width), jnp.float32),
                pltpu.VMEM((rows, 2), jnp.float32),
                pltpu.VMEM((rows, 2), jnp.int32),
                pltpu.VMEM((rows, width), jnp.float32),
                pltpu.VMEM((rows, width), jnp.bfloat16),
                pltpu.VMEM((rows, width), jnp.bfloat16),
                pltpu.VMEM((wide, width), jnp.bfloat16),
                pltpu.VMEM((wide, width), jnp.bfloat16),
                pltpu.VMEM((rows, width), jnp.float32),
            ] + route_scratch + [pltpu.SemaphoreType.DMA((6,))] + remote_sems,
            compiler_params=remote_params,
            name="layer",
        )(images, w_query, w_key, w_value, w_output, router_rows, route_rows, w_in, w_out)
    middle = attention_over_nodes(images, w_query, w_key, w_value, w_output)[0]
    middle = jnp.pad(middle, ((0, rows - tokens), (0, 0)))
    outgoing, gates, places = pl.pallas_call(
        functools.partial(route_kernel, tokens),
        out_shape=[blocks] + small,
        in_specs=[here] * 3,
        out_specs=[here] * 3,
        scratch_shapes=route_scratch,
        compiler_params=params,
        name="route",
    )(middle, router_rows, route_rows)
    returned = pl.pallas_call(
        functools.partial(expert_kernel, node_count, columns),
        out_shape=jax.ShapeDtypeStruct((number, CAP, width), jnp.bfloat16),
        in_specs=[here, anywhere, anywhere],
        out_specs=here,
        scratch_shapes=weight_scratch + [exchange_blocks] * 2 + [
            total_scratch,
            pltpu.SemaphoreType.DMA((2,)),
        ] + remote_sems,
        compiler_params=remote_params,
        name="experts",
    )(outgoing, w_in, w_out)
    me = lax.axis_index("node") * columns + lax.axis_index("ep")
    away = (jnp.arange(number) - me) % number
    step, ahead = away % (number // PLANES), away // (number // PLANES)
    returned = jnp.take(returned, step // 2 * CHUNK + (ahead + PLANES - 2) % PLANES * 2 + step % 2, axis=0)
    summed = jnp.sum(returned.astype(jnp.float32).reshape(node_count, experts, CAP, width), axis=0)
    return pl.pallas_call(
        functools.partial(combine_kernel, tokens),
        out_shape=jax.ShapeDtypeStruct(images.shape, jnp.bfloat16),
        in_specs=[here] * 4,
        out_specs=here,
        compiler_params=params,
        name="combine",
    )(middle, gates, places, summed.astype(jnp.bfloat16))


def solution(mesh):
    placed = (
        P(("node", "ep"), None, None),
        P(None, "node"),
        P(None, "node"),
        P(None, "node"),
        P(),
        P(),
        P("ep", None, "node"),
        P("ep", "node", None),
        P(("node", "ep"), None, None),
    )
    return jax.shard_map(
        shards, mesh=mesh, in_specs=placed, out_specs=P(("node", "ep"), None, None), check_vma=False
    )
```

```python
import functools
import math

import jax
import jax.numpy as jnp
from jax import lax
from jax.experimental import pallas as pl
from jax.experimental.pallas import tpu as pltpu
from jax.sharding import PartitionSpec as P

HEAD = 80
CAP = 24
LANES = 128
TILE = 256
PLANES = 4
CHUNK = 8
VMEM_BYTES = 60 * 1024 * 1024
MESH = pl.DeviceIdType.MESH


def up_to(value, step):
    return (value + step - 1) // step * step


def layer_norm(values):
    center = values - jnp.mean(values, axis=-1, keepdims=True)
    spread = jnp.mean(center * center, axis=-1, keepdims=True)
    return center * lax.rsqrt(spread + 1e-06)


def choose(rows, experts, routes, table, which):
    columns = lax.broadcasted_iota(jnp.int32, (rows, experts), 1)
    return jnp.sum(jnp.where(routes[:, which : which + 1] == columns, table, 0.0), axis=1, keepdims=True)


def route(tokens, rows, wide, router_ref, routes_ref, middle, gate_ref, place_ref, normed, wanted, turned):
    width = middle.shape[1]
    experts = router_ref.shape[0]
    normed[rows:, :] = jnp.zeros((wide - rows, width), jnp.bfloat16)
    normed[:rows, :] = layer_norm(middle[...]).astype(jnp.bfloat16)
    wanted[...] = jnp.full(wanted.shape, -1.0, jnp.float32)
    wanted[0:2, :tokens] = routes_ref[...].astype(jnp.float32)
    routes_wide = jnp.transpose(wanted[...]).astype(jnp.int32)
    logits = lax.dot_general(
        normed[...], router_ref[...], (((1,), (1,)), ((), ())), preferred_element_type=jnp.float32
    )
    columns = lax.broadcasted_iota(jnp.int32, (wide, experts), 1)
    named = jnp.where(routes_wide[:, 0:1] == columns, 1.0, 0.0) + jnp.where(
        routes_wide[:, 1:2] == columns, 1.0, 0.0
    )
    earlier = jnp.where(
        lax.broadcasted_iota(jnp.int32, (wide, wide), 1) < lax.broadcasted_iota(jnp.int32, (wide, wide), 0),
        1.0,
        0.0,
    ).astype(jnp.bfloat16)
    rank = jnp.dot(earlier, named.astype(jnp.bfloat16), preferred_element_type=jnp.float32)
    column = lax.broadcasted_iota(jnp.int32, (wide, 8), 1)
    both = jnp.full((wide, 8), -1.0, jnp.float32)
    for which in range(2):
        route_column = routes_wide[:, which : which + 1]
        gate_ref[:, which : which + 1] = jax.nn.sigmoid(
            choose(wide, experts, routes_wide, logits, which)[:rows, :]
        )
        turn = choose(wide, experts, routes_wide, rank, which).astype(jnp.int32)
        place = jnp.where(route_column >= 0, turned(route_column) * CAP + turn, -1)
        place_ref[:, which : which + 1] = place[:rows, :]
        both = jnp.where(column == which, place.astype(jnp.float32), both)
    return jnp.transpose(both).astype(jnp.int32)


def gather_rows(across, normed, start, blocks, out_ref, at):
    wide, width = normed.shape
    slot_of = lax.broadcasted_iota(jnp.int32, (blocks * CAP, wide), 0) + start
    picks = jnp.where(across[0:1, :] == slot_of, 1.0, 0.0) + jnp.where(across[1:2, :] == slot_of, 1.0, 0.0)
    picks = picks.astype(jnp.bfloat16)
    for tile in range(width // TILE):
        part = pl.ds(tile * TILE, TILE)
        block = jnp.dot(picks, normed[:, part], preferred_element_type=jnp.float32)
        out_ref[pl.ds(at, blocks), :, part] = block.reshape(blocks, CAP, TILE).astype(jnp.bfloat16)


def attend(tokens, images_ref, loads, weights, middle_ref, inputs, normed, queries, keys, values, mixed):
    rows, width = inputs.shape
    wide = keys.shape[0]
    inputs[...] = jnp.zeros((rows, width), jnp.float32)
    inputs[:tokens, :] = images_ref[0].astype(jnp.float32)
    normed[...] = layer_norm(inputs[...]).astype(jnp.bfloat16)
    mixed[...] = jnp.zeros((rows, width), jnp.float32)
    keys[rows:, :] = jnp.zeros((wide - rows, width), jnp.bfloat16)
    values[rows:, :] = jnp.zeros((wide - rows, width), jnp.bfloat16)
    for at, target in enumerate((queries, keys, values)):
        loads[at].wait()
        loads[at + 2].start()

        @pl.loop(0, width // TILE)
        def _(tile):
            part = pl.ds(pl.multiple_of(tile * TILE, TILE), TILE)
            taken = pl.ds(pl.multiple_of(at * width + tile * TILE, TILE), TILE)
            target[:rows, part] = jnp.dot(
                normed[...], weights[:, taken], preferred_element_type=jnp.float32
            ).astype(jnp.bfloat16)

    period = math.lcm(HEAD, LANES)
    valid = lax.broadcasted_iota(jnp.int32, (rows, wide), 1) < tokens

    for turn in range(width // period):
        for head in range(period // HEAD):
            low = head * HEAD // LANES * LANES
            span = up_to(head * HEAD + HEAD, LANES) - low
            part = pl.ds(turn * period + low, span)
            lane = lax.broadcasted_iota(jnp.int32, (rows, span), 1) + low
            inside = (lane >= head * HEAD) & (lane < head * HEAD + HEAD)
            query = jnp.where(inside, queries[:, part].astype(jnp.float32), 0.0).astype(jnp.bfloat16)
            scores = lax.dot_general(
                query, keys[:, part], (((1,), (1,)), ((), ())), preferred_element_type=jnp.float32
            ) * (1.0 / math.sqrt(HEAD))
            scores = jnp.where(valid, scores, -1e30)
            raised = jnp.exp(scores - jnp.max(scores, axis=1, keepdims=True))
            probs = (raised * (1.0 / jnp.sum(raised, axis=1, keepdims=True))).astype(jnp.bfloat16)
            result = jnp.dot(probs, values[:, part], preferred_element_type=jnp.float32)
            mixed[:, part] += jnp.where(inside, result, 0.0)

    normed[...] = mixed[...].astype(jnp.bfloat16)
    loads[3].wait()

    @pl.loop(0, width // TILE)
    def _(tile):
        part = pl.ds(pl.multiple_of(tile * TILE, TILE), TILE)
        taken = pl.ds(pl.multiple_of(3 * width + tile * TILE, TILE), TILE)
        middle_ref[:, part] = inputs[:, part] + jnp.dot(
            normed[...], weights[:, taken], preferred_element_type=jnp.float32
        )


def route_kernel(tokens, middle_ref, router_ref, routes_ref, out_ref, gate_ref, place_ref, second, wanted):
    rows, wide = middle_ref.shape[0], second.shape[0]
    across = route(
        tokens, rows, wide, router_ref, routes_ref, middle_ref, gate_ref, place_ref, second, wanted,
        lambda expert: expert,
    )

    @pl.loop(0, out_ref.shape[0] // CHUNK)
    def _(chunk):
        gather_rows(across, second, chunk * CHUNK * CAP, CHUNK, out_ref, chunk * CHUNK)


def place_of(node_count, columns):
    return lax.axis_index("node") * columns + lax.axis_index("ep")


def greet(node_count, columns):
    number = node_count * columns
    me = place_of(node_count, columns)
    barrier = pltpu.get_barrier_semaphore()

    @pl.loop(1, number)
    def _(step):
        peer = (me + step) % number
        pl.semaphore_signal(
            barrier, inc=1, device_id=(peer // columns, peer % columns), device_id_type=MESH
        )

    return lambda: pl.semaphore_wait(barrier, number - 1)


def exchange(
    node_count, columns, out_ref, loads, back_ref,
    first, second, arrived, results, total, go_send, go_recv, back_send, back_recv, given=None, taken=None,
):
    number = node_count * columns
    plane = number // PLANES
    chunks = number // CHUNK
    own_slot = 4
    me = place_of(node_count, columns)

    def offset(slot):
        within = slot % CHUNK
        return (within // 2 + 2) % PLANES * plane + slot // CHUNK * 2 + within % 2

    def name(device):
        return (device // columns, device % columns)

    def go(slot):
        target = (me + offset(slot)) % number
        return pltpu.make_async_remote_copy(
            src_ref=out_ref.at[target % columns if given is None else slot],
            dst_ref=arrived.at[slot],
            send_sem=go_send.at[slot],
            recv_sem=go_recv.at[slot],
            device_id=name(target),
            device_id_type=MESH,
        )

    def back(slot):
        source = (me - offset(slot) + number) % number
        return pltpu.make_async_remote_copy(
            src_ref=results.at[slot],
            dst_ref=back_ref.at[slot],
            send_sem=back_send.at[slot],
            recv_sem=back_recv.at[slot],
            device_id=name(source),
            device_id_type=MESH,
        )

    def landed(slot):
        source = (me + offset(slot)) % number
        return pltpu.make_async_remote_copy(
            src_ref=results.at[slot],
            dst_ref=back_ref.at[slot],
            send_sem=back_send.at[slot],
            recv_sem=back_recv.at[slot],
            device_id=name(source),
            device_id_type=MESH,
        )

    @pl.loop(0, chunks)
    def _(chunk):
        if given is not None:
            given(chunk)
        for within in range(CHUNK):
            slot = chunk * CHUNK + within

            @pl.when(slot != own_slot)
            def _():
                go(slot).start()

    arrived[own_slot] = out_ref[me % columns if given is None else own_slot]
    for load in loads:
        load.wait()
    width, hidden_units = first.shape
    section = width if hidden_units % width == 0 else hidden_units

    @pl.loop(0, chunks)
    def _(chunk):
        for within in range(CHUNK):
            slot = chunk * CHUNK + within

            @pl.when(slot != own_slot)
            def _():
                go(slot).wait_recv()

        held = pl.ds(chunk * CHUNK, CHUNK)
        buffer = arrived[held].astype(jnp.float32).reshape(CHUNK * CAP, width).astype(jnp.bfloat16)
        total[...] = jnp.zeros_like(total)

        @pl.loop(0, hidden_units // section)
        def _(at):
            part = pl.ds(pl.multiple_of(at * section, section), section)
            before = jnp.dot(buffer, first[:, part], preferred_element_type=jnp.float32)
            hidden = jax.nn.gelu(before, approximate=True).astype(jnp.bfloat16)
            total[...] += jnp.dot(hidden, second[part, :], preferred_element_type=jnp.float32)

        results[held] = total[...].reshape(CHUNK, CAP, width).astype(jnp.bfloat16)
        for within in range(CHUNK):
            slot = chunk * CHUNK + within

            @pl.when(slot != own_slot)
            def _():
                back(slot).start()

    back_ref[own_slot] = results[own_slot]

    @pl.loop(0, chunks)
    def _(chunk):
        for within in range(CHUNK):
            slot = chunk * CHUNK + within

            @pl.when(slot != own_slot)
            def _():
                landed(slot).wait_recv()

        if taken is not None:
            taken(chunk)

    @pl.loop(0, number)
    def _(slot):
        @pl.when(slot != own_slot)
        def _():
            go(slot).wait_send()
            back(slot).wait_send()


def slot_for(expert, me, columns):
    plane = columns // PLANES
    away = (expert - me + columns) & (columns - 1)
    ahead, step = away // plane, away & (plane - 1)
    return step // 2 * CHUNK + ((ahead + PLANES - 2) & (PLANES - 1)) * 2 + (step & 1)


def layer_kernel(
    tokens, columns, images_ref, q_hbm, k_hbm, v_hbm, o_hbm, router_ref, routes_ref, in_hbm, down_hbm, result_ref,
    first, second, outgoing, arrived, results, returned, total, middle, gates, places,
    inputs, normed, queries, keys, values, mixed, normed_second, wanted,
    load_sems, go_send, go_recv, back_send, back_recv,
):
    rows, width = inputs.shape
    wide = keys.shape[0]
    loads = [
        pltpu.make_async_copy(source, first.at[:, pl.ds(at * width, width)], load_sems.at[at])
        for at, source in enumerate((q_hbm, k_hbm, v_hbm, o_hbm))
    ]
    for load in loads[:2]:
        load.start()
    down = pltpu.make_async_copy(down_hbm.at[0], second, load_sems.at[4])
    up = pltpu.make_async_copy(in_hbm.at[0], first, load_sems.at[5])
    met = greet(1, columns)
    attend(tokens, images_ref, loads + [down], first, middle, inputs, normed, queries, keys, values, mixed)
    up.start()
    me = place_of(1, columns)
    across = route(
        tokens, rows, wide, router_ref, routes_ref, middle, gates, places, normed_second, wanted,
        lambda expert: slot_for(expert, me, columns),
    )
    met()
    span = CHUNK * CAP

    def given(chunk):
        gather_rows(across, normed_second, chunk * span, CHUNK, outgoing, chunk * CHUNK)

    def taken(chunk):
        column = lax.broadcasted_iota(jnp.int32, (rows, span), 1) + chunk * span
        picks = [
            jnp.where(places[:, which : which + 1] == column, 1.0, 0.0).astype(jnp.bfloat16)
            for which in range(2)
        ]
        blocks = returned[pl.ds(chunk * CHUNK, CHUNK)].astype(jnp.float32)
        blocks = blocks.reshape(span, width).astype(jnp.bfloat16)
        for tile in range(width // TILE):
            part = pl.ds(tile * TILE, TILE)
            mix = middle[:, part]
            for which in range(2):
                mix = mix + gates[:, which : which + 1] * jnp.dot(
                    picks[which], blocks[:, tile * TILE : (tile + 1) * TILE], preferred_element_type=jnp.float32
                )
            middle[:, part] = mix

    exchange(
        1, columns, outgoing, [down, up], returned,
        first, second, arrived, results, total, go_send, go_recv, back_send, back_recv, given, taken,
    )
    result_ref[0] = middle[:tokens, :].astype(jnp.bfloat16)


def expert_kernel(
    node_count, columns, out_ref, in_hbm, down_hbm, back_ref,
    first, second, arrived, results, total, load_sems, go_send, go_recv, back_send, back_recv,
):
    loads = [
        pltpu.make_async_copy(in_hbm.at[0], first, load_sems.at[0]),
        pltpu.make_async_copy(down_hbm.at[0], second, load_sems.at[1]),
    ]
    for load in loads:
        load.start()
    greet(node_count, columns)()
    exchange(
        node_count, columns, out_ref, loads, back_ref,
        first, second, arrived, results, total, go_send, go_recv, back_send, back_recv,
    )


def combine_kernel(tokens, middle_ref, gate_ref, place_ref, back_ref, out_ref):
    rows, width = middle_ref.shape
    experts = back_ref.shape[0]
    slots = experts * CAP
    slot_of = lax.broadcasted_iota(jnp.int32, (rows, slots), 1)
    picks = [
        jnp.where(place_ref[:, which : which + 1] == slot_of, 1.0, 0.0).astype(jnp.bfloat16)
        for which in range(2)
    ]

    @pl.loop(0, width // TILE)
    def _(tile):
        part = pl.ds(pl.multiple_of(tile * TILE, TILE), TILE)
        block = back_ref[:, :, part].astype(jnp.float32).reshape(slots, TILE).astype(jnp.bfloat16)
        value = middle_ref[:, part]
        mix = jnp.zeros_like(value)
        for which in range(2):
            mix = mix + gate_ref[:, which : which + 1] * jnp.dot(
                picks[which], block, preferred_element_type=jnp.float32
            )
        out_ref[0, :, part] = (value + mix)[:tokens, :].astype(jnp.bfloat16)


def attention_over_nodes(images, w_query, w_key, w_value, w_output):
    local_heads = w_query.shape[1] // HEAD
    inputs = images.astype(jnp.float32)
    normed = layer_norm(inputs).astype(jnp.bfloat16)
    gathered = lax.all_gather(normed, "node", axis=0, tiled=True)
    number, tokens, _ = gathered.shape

    def project(weight):
        result = jnp.einsum("ctd,de->cte", gathered, weight, preferred_element_type=jnp.float32)
        return result.astype(jnp.bfloat16).reshape(number, tokens, local_heads, HEAD)

    scores = jnp.einsum(
        "cqhd,ckhd->chqk", project(w_query), project(w_key), preferred_element_type=jnp.float32
    ) / math.sqrt(HEAD)
    probs = jax.nn.softmax(scores, axis=-1).astype(jnp.bfloat16)
    mixture = jnp.einsum(
        "chqk,ckhd->cqhd", probs, project(w_value), preferred_element_type=jnp.float32
    ).astype(jnp.bfloat16)
    mixture = mixture.reshape(number, tokens, local_heads * HEAD)
    mixture = lax.all_to_all(mixture, "node", split_axis=0, concat_axis=2, tiled=True)
    return inputs + jnp.einsum("itd,de->ite", mixture, w_output, preferred_element_type=jnp.float32)


def shards(images, w_query, w_key, w_value, w_output, router, w_in, w_out, routes):
    _, tokens, width = images.shape
    node_count = lax.axis_size("node")
    columns = lax.axis_size("ep")
    number = node_count * columns
    experts = router.shape[1]
    hidden_units = w_in.shape[2]
    rows, wide = up_to(tokens, 16), up_to(tokens, LANES)
    here = pl.BlockSpec(memory_space=pltpu.VMEM)
    anywhere = pl.BlockSpec(memory_space=pl.ANY)
    params = pltpu.CompilerParams(vmem_limit_bytes=VMEM_BYTES)
    blocks = jax.ShapeDtypeStruct((experts, CAP, width), jnp.bfloat16)
    middle_shape = jax.ShapeDtypeStruct((rows, width), jnp.float32)
    small = [jax.ShapeDtypeStruct((rows, 2), jnp.float32), jax.ShapeDtypeStruct((rows, 2), jnp.int32)]
    route_scratch = [pltpu.VMEM((wide, width), jnp.bfloat16), pltpu.VMEM((8, wide), jnp.float32)]
    exchange_blocks = pltpu.VMEM((number, CAP, width), jnp.bfloat16)
    weight_scratch = [
        pltpu.VMEM((width, hidden_units), jnp.bfloat16),
        pltpu.VMEM((hidden_units, width), jnp.bfloat16),
    ]
    total_scratch = pltpu.VMEM((CHUNK * CAP, width), jnp.float32)
    remote_sems = [pltpu.SemaphoreType.DMA((number,))] * 4
    remote_params = pltpu.CompilerParams(
        collective_id=0, has_side_effects=True, vmem_limit_bytes=VMEM_BYTES
    )
    router_rows, route_rows = router.T, routes[0].T
    if node_count == 1 and hidden_units >= 4 * width:
        return pl.pallas_call(
            functools.partial(layer_kernel, tokens, columns),
            out_shape=jax.ShapeDtypeStruct(images.shape, jnp.bfloat16),
            in_specs=[here] + [anywhere] * 4 + [here] * 2 + [anywhere] * 2,
            out_specs=here,
            scratch_shapes=weight_scratch + [exchange_blocks] * 4 + [
                total_scratch,
                pltpu.VMEM((rows, width), jnp.float32),
                pltpu.VMEM((rows, 2), jnp.float32),
                pltpu.VMEM((rows, 2), jnp.int32),
                pltpu.VMEM((rows, width), jnp.float32),
                pltpu.VMEM((rows, width), jnp.bfloat16),
                pltpu.VMEM((rows, width), jnp.bfloat16),
                pltpu.VMEM((wide, width), jnp.bfloat16),
                pltpu.VMEM((wide, width), jnp.bfloat16),
                pltpu.VMEM((rows, width), jnp.float32),
            ] + route_scratch + [pltpu.SemaphoreType.DMA((6,))] + remote_sems,
            compiler_params=remote_params,
            name="layer",
        )(images, w_query, w_key, w_value, w_output, router_rows, route_rows, w_in, w_out)
    middle = attention_over_nodes(images, w_query, w_key, w_value, w_output)[0]
    middle = jnp.pad(middle, ((0, rows - tokens), (0, 0)))
    outgoing, gates, places = pl.pallas_call(
        functools.partial(route_kernel, tokens),
        out_shape=[blocks] + small,
        in_specs=[here] * 3,
        out_specs=[here] * 3,
        scratch_shapes=route_scratch,
        compiler_params=params,
        name="route",
    )(middle, router_rows, route_rows)
    returned = pl.pallas_call(
        functools.partial(expert_kernel, node_count, columns),
        out_shape=jax.ShapeDtypeStruct((number, CAP, width), jnp.bfloat16),
        in_specs=[here, anywhere, anywhere],
        out_specs=here,
        scratch_shapes=weight_scratch + [exchange_blocks] * 2 + [
            total_scratch,
            pltpu.SemaphoreType.DMA((2,)),
        ] + remote_sems,
        compiler_params=remote_params,
        name="experts",
    )(outgoing, w_in, w_out)
    me = lax.axis_index("node") * columns + lax.axis_index("ep")
    away = (jnp.arange(number) - me) % number
    step, ahead = away % (number // PLANES), away // (number // PLANES)
    returned = jnp.take(returned, step // 2 * CHUNK + (ahead + PLANES - 2) % PLANES * 2 + step % 2, axis=0)
    summed = jnp.sum(returned.astype(jnp.float32).reshape(node_count, experts, CAP, width), axis=0)
    return pl.pallas_call(
        functools.partial(combine_kernel, tokens),
        out_shape=jax.ShapeDtypeStruct(images.shape, jnp.bfloat16),
        in_specs=[here] * 4,
        out_specs=here,
        compiler_params=params,
        name="combine",
    )(middle, gates, places, summed.astype(jnp.bfloat16))


def solution(mesh):
    placed = (
        P(("node", "ep"), None, None),
        P(None, "node"),
        P(None, "node"),
        P(None, "node"),
        P(),
        P(),
        P("ep", None, "node"),
        P("ep", "node", None),
        P(("node", "ep"), None, None),
    )
    return jax.shard_map(
        shards, mesh=mesh, in_specs=placed, out_specs=P(("node", "ep"), None, None), check_vma=False
    )
```
